512 devices in a mesh: band: 32 (over z, y_lo), grid: 16 (over x, y_hi, core).
Axes of the slice: x: 4, y: 4 (y_hi: 2, y_lo: 2; y = y_hi * 2 + y_lo), z: 16, core: 2. Of those that a mesh axis runs over, the one named last changes fastest.
Arguments:
- orbitals: float32 [64, 96, 96, 128], P('band', 'grid'), may hold values from -6 to 6
- kernel: float32 [96, 96, 128], P(None, 'grid'), as said below
- owners: int32 [1], replicated, may hold values from 0 to 31
Outputs:
- exchange_applied: float32 [64, 96, 96, 128], P('band', 'grid')
The draws below stay inside these ranges and needn't reach their ends.
Inputs may be any that keep to these rules, and one draw needn't show every extreme that they name: kernel is zero at the zero frequency, positive elsewhere, and even: its value at indices (a, b, c) equals that at ((-a) mod 96, (-b) mod 96, (-c) mod 128).
All inputs are finite; a program needn't handle non-finite values.
Results may differ from the reference program's by a relative error of at most 0.0003.
Values sent between devices are 32-bit elements; how exact they have to be, the bound alone decides.
No kernel may reach another device: no remote copies, remote signals or barrier semaphores. Data moves between devices by JAX's collectives and lax.ppermute only.
A program may use at most 64 MiB of HBM per device.

```python
import jax
import jax.numpy as jnp
from jax import lax

NX = 96
NY = 96
NZ = 128
ORB_DEV = 2
STEPS = 1
ORBITALS = 64
N_BAND = 32


def wave_square(length, aspect_value):
    counter = jnp.arange(length, dtype=jnp.int32)
    signed = jnp.where(counter > length // 2, counter - length, counter).astype(jnp.float32)
    return (2.0 * signed / (length * aspect_value)) ** 2


def draw_kernel(key, part):
    key = jax.random.fold_in(key, 7)
    subkeys = jax.random.split(key, 4)
    lowest, highest, stretch = (0.01, 0.05, 0.25)
    screening = jnp.exp(jax.random.uniform(subkeys[0], (), jnp.float32, jnp.log(lowest), jnp.log(highest)))
    aspect_x = jnp.exp(jax.random.uniform(subkeys[1], (), jnp.float32, -stretch, stretch))
    aspect_y = jnp.exp(jax.random.uniform(subkeys[2], (), jnp.float32, -stretch, stretch))
    aspect_z = jnp.exp(jax.random.uniform(subkeys[3], (), jnp.float32, -stretch, stretch))
    square_x = wave_square(NX, aspect_x)
    square_y = wave_square(NY, aspect_y)
    square_z = wave_square(NZ, aspect_z)
    summed = square_x[:, None, None] + square_y[None, :, None] + square_z[None, None, :]
    values = 0.4 / (summed + screening * screening)
    index_x = jnp.arange(NX, dtype=jnp.int32)[:, None, None]
    index_y = jnp.arange(NY, dtype=jnp.int32)[None, :, None]
    index_z = jnp.arange(NZ, dtype=jnp.int32)[None, None, :]
    anchor = index_x + index_y + index_z == 0
    return jnp.where(anchor, 0.0, values).astype(jnp.float32)


def shard_levels(stream_key, shape, shards, least, high):
    def one(axis_at, blocks):
        steps = jax.random.uniform(jax.random.fold_in(jax.random.fold_in(stream_key, 6), axis_at), (blocks,), jnp.float32, least / len(shards), high / len(shards))
        return jnp.repeat(jnp.exp(steps), shape[axis_at] // blocks).reshape((-1,) + (1,) * (len(shape) - axis_at - 1))

    level = one(*shards[0])
    for cut in shards[1:]:
        level = level * one(*cut)
    return level


def centred(stream_key, shape, width, limit, cuts=(), held_as=jnp.bfloat16):
    drawn = width * jax.random.normal(stream_key, shape, jnp.float32)
    if cuts:
        drawn = drawn * shard_levels(stream_key, shape, cuts, -0.22, 0.18)
    return jnp.clip(drawn, -limit, limit).astype(held_as)


def setup_inputs(seed: int = 0) -> dict:
    key_list = jax.random.split(jax.random.key(seed), 4)
    orbitals = centred(key_list[0], (ORBITALS, NX, NY, NZ), 1.0, 6.0, ((0, 32), (1, 16)), jnp.float32)
    kernel = draw_kernel(jax.random.fold_in(key_list[3], 71), 0)
    owners = jax.random.randint(key_list[2], (STEPS,), 0, N_BAND).astype(jnp.int32)
    return {"orbitals": orbitals, "kernel": kernel, "owners": owners}


def reference(orbitals, kernel, owners):
    half_kernel = kernel[:, :, : NZ // 2 + 1]

    def one_orbital(resident):
        accumulated = jnp.zeros_like(resident)
        for number in range(STEPS):
            start = owners[number].astype(jnp.int32) * ORB_DEV
            source_block = lax.dynamic_slice_in_dim(orbitals, start, ORB_DEV, 0)

            def add_pair(carry, partner):
                density = resident * partner
                spectrum = jnp.fft.rfftn(density) * half_kernel
                potential = jnp.fft.irfftn(spectrum, s=(NX, NY, NZ)).astype(resident.dtype)
                return carry + partner * potential, None

            accumulated = lax.scan(add_pair, accumulated, source_block)[0]
        return -0.25 * accumulated

    return lax.map(one_orbital, orbitals)
```

```python
import math

import jax
import jax.numpy as jnp
from jax import lax
from jax.sharding import Mesh, PartitionSpec as P

precise = lax.Precision.HIGH
mixing = 0.25
band_axes = ("z", "y_lo")
grid_axes = ("x", "y_hi", "core")


def broadcast(block, holder):
    planes, pair = lax.axis_size("z"), lax.axis_size("y_lo")
    holder_z, holder_y = holder // pair, holder % pair
    mine = lax.axis_index("y_lo")
    rows = block.reshape(pair, planes, -1, block.shape[-1])
    swap = [(0, 1), (1, 0)]
    kept = lax.dynamic_index_in_dim(rows, mine, 0, keepdims=False)
    other = lax.dynamic_index_in_dim(rows, 1 - mine, 0, keepdims=False)
    received = lax.ppermute(other, "y_lo", swap)
    half = jnp.where(mine == holder_y, kept, received)
    pieces = lax.all_to_all(half, "z", 0, 0, tiled=True)
    piece = lax.dynamic_index_in_dim(pieces, holder_z, 0, keepdims=True)
    half = lax.all_to_all(jnp.broadcast_to(piece, half.shape), "z", 0, 0, tiled=True)
    partner = lax.ppermute(half, "y_lo", swap)
    low = jnp.where(mine == 0, half, partner)
    high = jnp.where(mine == 0, partner, half)
    return jnp.stack([low, high]).reshape(block.shape)


def twiddle(length):
    counter = jnp.arange(length, dtype=jnp.int32)
    phases = counter[:, None] * counter[None, :] % length
    angles = phases.astype(jnp.float32) * (2.0 * math.pi / length)
    return (jnp.cos(angles), jnp.sin(angles))


def along_dim(spectrum, cosine, sine_part, letters, forward):
    with_cosine = jnp.einsum(
        letters, cosine, spectrum, precision=precise, preferred_element_type=jnp.float32
    )
    with_sine = jnp.einsum(
        letters, sine_part, spectrum, precision=precise, preferred_element_type=jnp.float32
    )
    middle = spectrum.shape[-1] // 2
    real_cosine, imag_cosine = (with_cosine[..., :middle], with_cosine[..., middle:])
    real_sine, imag_sine = (with_sine[..., :middle], with_sine[..., middle:])
    if forward:
        return jnp.concatenate([real_cosine + imag_sine, imag_cosine - real_sine], axis=-1)
    return jnp.concatenate([real_cosine - imag_sine, imag_cosine + real_sine], axis=-1)


def local(orbitals, kernel, owners):
    orb_count, slab_x, rows_y, cells_z = orbitals.shape
    full_x = slab_x * lax.axis_size(grid_axes)
    cosine_x, sine_x = twiddle(full_x)
    cosine_y, sine_y = twiddle(rows_y)
    cosine_z, sine_z = twiddle(cells_z)
    norm_scale = 1.0 / (full_x * rows_y * cells_z)
    kernel_pair = jnp.concatenate([kernel, kernel], axis=-1)
    wave_z = jnp.concatenate(
        [
            jnp.concatenate([cosine_z, -sine_z], axis=1),
            jnp.concatenate([sine_z, cosine_z], axis=1),
        ],
        axis=0,
    )
    source_block = broadcast(orbitals, owners[0])
    density = jnp.concatenate(
        [orbitals * source_block[0][None], orbitals * source_block[1][None]], axis=-1
    )
    spectrum = jnp.dot(density, wave_z, precision=precise, preferred_element_type=jnp.float32)
    spectrum = along_dim(spectrum, cosine_y, sine_y, "ky,bxyc->bxkc", True)
    columns = lax.all_to_all(spectrum, grid_axes, split_axis=2, concat_axis=1, tiled=True)
    spectral_spectrum = along_dim(columns, cosine_x, sine_x, "kx,bxyc->bkyc", True)
    spectral_spectrum = spectral_spectrum * kernel_pair
    spectral_spectrum = along_dim(spectral_spectrum, cosine_x, sine_x, "kx,bxyc->bkyc", False)
    spectrum = lax.all_to_all(spectral_spectrum, grid_axes, split_axis=1, concat_axis=2, tiled=True)
    spectrum = along_dim(spectrum, cosine_y, sine_y, "ky,bxyc->bxkc", False)
    potential = jnp.dot(
        spectrum, wave_z.T * norm_scale, precision=precise, preferred_element_type=jnp.float32
    )
    accumulated = (
        source_block[0][None] * potential[..., :cells_z]
        + source_block[1][None] * potential[..., cells_z:]
    )
    return -mixing * accumulated


def solution(mesh):
    pair = 2
    band, grid = mesh.shape["band"], mesh.shape["grid"]
    shape = (band // pair, pair, grid // (2 * pair), pair, 2)
    fine = Mesh(mesh.devices.reshape(shape), band_axes + grid_axes)
    return jax.shard_map(
        local,
        mesh=fine,
        in_specs=(P(band_axes, grid_axes, None, None), P(None, grid_axes, None), P()),
        out_specs=P(band_axes, grid_axes, None, None),
        check_vma=False,
    )
```

```python
import functools

import jax
import jax.numpy as jnp
import numpy as np
from jax import lax
from jax.experimental import pallas as pl
from jax.experimental.pallas import tpu as pltpu
from jax.sharding import Mesh, PartitionSpec as P

mixing = 0.25
pair = 2
far_axis = "z_far"
near_axes = ("z_near", "y_lo")
band_axes = (far_axis,) + near_axes
grid_axes = ("x", "y_hi", "core")
lanes = 128


def pieces_of(block, axes, holder):
    pieces = block.reshape(lax.axis_size(axes), -1, block.shape[-1])
    received = lax.all_to_all(pieces, axes, 0, 0, tiled=True)
    return lax.dynamic_index_in_dim(received, holder, 0, keepdims=False)


def copies_of(piece, axes):
    copies = jnp.broadcast_to(piece[None], (lax.axis_size(axes),) + piece.shape)
    return lax.all_to_all(copies, axes, 0, 0, tiled=True)


def broadcast(block, holder):
    members = lax.axis_size(near_axes)
    piece = pieces_of(block, near_axes, holder % members)
    everywhere = copies_of(piece, far_axis)
    piece = lax.dynamic_index_in_dim(everywhere, holder // members, 0, keepdims=False)
    return copies_of(piece, near_axes).reshape(block.shape)


def wave(length, forward):
    counter = np.arange(length)
    angles = 2.0 * np.pi * (np.outer(counter, counter) % length) / length
    cosine, sine = np.cos(angles), np.sin(angles)
    if not forward:
        sine = -sine
    return np.block([[cosine, sine], [-sine, cosine]])


def spread(length, parts):
    order = np.arange(length).reshape(parts, -1).T.reshape(-1)
    return np.concatenate([order, order + length])


def halves(matrix):
    upper = matrix.astype(jnp.bfloat16)
    return upper, (matrix - upper.astype(np.float64)).astype(jnp.bfloat16)


def split(values):
    upper = values.astype(jnp.bfloat16)
    return upper, (values - upper.astype(jnp.float32)).astype(jnp.bfloat16)


def times(left, right):
    dot = functools.partial(jnp.dot, preferred_element_type=jnp.float32)
    return dot(left[0], right[0]) + dot(left[0], right[1]) + dot(left[1], right[0])


def both(pair_refs):
    return pair_refs[0][...], pair_refs[1][...]


def at(column):
    return slice(column * lanes, (column + 1) * lanes)


def to_columns(parts, orbitals, block, z_up, z_low, y_up, y_low, sent):
    orb_count, slab, rows, _ = orbitals.shape
    share = rows // parts
    stride = sent.shape[0] // parts
    wave_z, wave_y = both((z_up, z_low)), both((y_up, y_low))
    for orb in range(orb_count):
        density = jnp.concatenate([orbitals[orb] * block[0], orbitals[orb] * block[1]], axis=-1)
        spectrum = times(split(density.reshape(slab * rows, 2 * lanes)), wave_z)
        spectrum = spectrum.reshape(slab, rows, 2 * lanes)
        stacked = jnp.concatenate(
            [
                jnp.concatenate([spectrum[plane, :, :lanes], spectrum[plane, :, lanes:]], axis=0)
                for plane in range(slab)
            ],
            axis=1,
        )
        columns = times(wave_y, split(stacked))
        for part in range(2):
            for plane in range(slab):
                first = ((orb * 2 + part) * slab + plane) * share
                for place in range(share):
                    start = (part * share + place) * parts
                    sent[pl.ds(first + place, parts, stride), :] = columns[
                        start : start + parts, at(plane)
                    ]


def in_columns(parts, received, weights, f_up, f_low, i_up, i_low, sent):
    stride = received.shape[0] // parts
    group = f_up.shape[0] // parts
    share = weights.shape[1] // lanes
    forward, inverse = both((f_up, f_low)), both((i_up, i_low))
    scale = jnp.concatenate([weights[...]] * 2, axis=0)
    for orb in range(stride // (group * share)):
        first = orb * group * share
        stacked = jnp.concatenate(
            [
                jnp.concatenate(
                    [
                        received[pl.ds(first + row * share + place, parts, stride), :]
                        for place in range(share)
                    ],
                    axis=1,
                )
                for row in range(group)
            ],
            axis=0,
        )
        spectral = times(forward, split(stacked)) * scale
        planes = times(inverse, split(spectral))
        for row in range(group):
            for place in range(share):
                sent[pl.ds(first + row * share + place, parts, stride), :] = planes[
                    row * parts : (row + 1) * parts, at(place)
                ]


def from_columns(parts, received, block, y_up, y_low, z_up, z_low, out):
    orb_count, slab, rows, _ = out.shape
    share = rows // parts
    stride = received.shape[0] // parts
    wave_y, wave_z = both((y_up, y_low)), both((z_up, z_low))
    for orb in range(orb_count):
        stacked = jnp.concatenate(
            [
                jnp.concatenate(
                    [
                        received[
                            pl.ds(
                                ((orb * 2 + part) * slab + plane) * share + place, parts, stride
                            ),
                            :,
                        ]
                        for part in range(2)
                        for place in range(share)
                    ],
                    axis=0,
                )
                for plane in range(slab)
            ],
            axis=1,
        )
        spectrum = times(wave_y, split(stacked))
        spectrum = jnp.concatenate(
            [
                jnp.concatenate([spectrum[:rows, at(plane)], spectrum[rows:, at(plane)]], axis=1)
                for plane in range(slab)
            ],
            axis=0,
        )
        potential = times(split(spectrum), wave_z).reshape(slab, rows, 2 * lanes)
        out[orb] = block[0] * potential[..., :lanes] + block[1] * potential[..., lanes:]


def on_device(body, shape, flops, *operands):
    moved = sum(x.size * x.dtype.itemsize for x in operands) + 4 * int(np.prod(shape))
    return pl.pallas_call(
        body,
        out_shape=jax.ShapeDtypeStruct(shape, jnp.float32),
        in_specs=[pl.BlockSpec(memory_space=pltpu.VMEM)] * len(operands),
        out_specs=pl.BlockSpec(memory_space=pltpu.VMEM),
        compiler_params=pltpu.CompilerParams(vmem_limit_bytes=32 * 1024 * 1024),
        cost_estimate=pl.CostEstimate(flops=flops, bytes_accessed=moved, transcendentals=0),
    )(*operands)


def local(orbitals, kernel, owners):
    orb_count, slab, rows, cells = orbitals.shape
    parts = lax.axis_size(grid_axes)
    full = slab * parts
    share = rows // parts
    order_x, order_y = spread(full, parts), spread(rows, parts)
    forward_z = halves(wave(cells, True).T)
    inverse_z = halves(wave(cells, False).T * (-mixing / (full * rows * cells)))
    forward_y = halves(wave(rows, True)[order_y])
    inverse_y = halves(wave(rows, False)[:, order_y])
    forward_x = halves(wave(full, True)[order_x][:, order_x])
    inverse_x = halves(wave(full, False)[order_x][:, order_x])
    weights = kernel.reshape(parts, slab, share * cells).swapaxes(0, 1).reshape(full, share * cells)

    source_block = broadcast(orbitals, owners[0])
    sent_rows = orb_count * 2 * slab * share
    shape = (parts * sent_rows, cells)
    points = orb_count * slab * rows * cells

    def exchange(columns):
        columns = columns.reshape(parts, sent_rows, cells)
        return lax.all_to_all(columns, grid_axes, 0, 0, tiled=True).reshape(shape)

    columns = on_device(
        functools.partial(to_columns, parts),
        shape,
        24 * points * (cells + rows),
        orbitals,
        source_block,
        *forward_z,
        *forward_y,
    )
    columns = exchange(columns)
    columns = on_device(
        functools.partial(in_columns, parts),
        shape,
        48 * points * full,
        columns,
        weights,
        *forward_x,
        *inverse_x,
    )
    columns = exchange(columns)
    return on_device(
        functools.partial(from_columns, parts),
        orbitals.shape,
        24 * points * (cells + rows),
        columns,
        source_block,
        *inverse_y,
        *inverse_z,
    )


def solution(mesh):
    band, grid = mesh.shape["band"], mesh.shape["grid"]
    shape = (band // (4 * pair), 4, pair, grid // (2 * pair), pair, 2)
    fine = Mesh(mesh.devices.reshape(shape), band_axes + grid_axes)
    return jax.shard_map(
        local,
        mesh=fine,
        in_specs=(P(band_axes, grid_axes, None, None), P(None, grid_axes, None), P()),
        out_specs=P(band_axes, grid_axes, None, None),
        check_vma=False,
    )
```

```python
import functools

import jax
import jax.numpy as jnp
import numpy as np
from jax import lax
from jax.experimental import pallas as pl
from jax.experimental.pallas import tpu as pltpu
from jax.sharding import Mesh, PartitionSpec as P

mixing = 0.25
pair = 2
far_axis = "z_far"
near_axes = ("z_near", "y_lo")
band_axes = (far_axis,) + near_axes
grid_axes = ("x", "y_hi", "core")
lanes = 128


def pieces_of(block, axes, holder):
    pieces = block.reshape(lax.axis_size(axes), -1, block.shape[-1])
    received = lax.all_to_all(pieces, axes, 0, 0, tiled=True)
    return lax.dynamic_index_in_dim(received, holder, 0, keepdims=False)


def copies_of(piece, axes):
    copies = jnp.broadcast_to(piece[None], (lax.axis_size(axes),) + piece.shape)
    return lax.all_to_all(copies, axes, 0, 0, tiled=True)


def broadcast(block, holder, aside):
    members = lax.axis_size(near_axes)
    piece = pieces_of(block, near_axes, holder % members)
    piece, aside = lax.optimization_barrier((piece, aside))
    everywhere = lax.all_gather(piece, far_axis, axis=0)
    piece = lax.dynamic_index_in_dim(everywhere, holder // members, 0, keepdims=False)
    return copies_of(piece, near_axes).reshape(block.shape), aside


def wave(length, forward):
    counter = np.arange(length)
    angles = 2.0 * np.pi * (np.outer(counter, counter) % length) / length
    cosine, sine = np.cos(angles), np.sin(angles)
    if not forward:
        sine = -sine
    return np.block([[cosine, sine], [-sine, cosine]])


def spread(length, parts):
    order = np.arange(length).reshape(parts, -1).T.reshape(-1)
    return np.concatenate([order, order + length])


def halves(matrix):
    upper = matrix.astype(jnp.bfloat16)
    return upper, (matrix - upper.astype(np.float64)).astype(jnp.bfloat16)


def split(values):
    upper = values.astype(jnp.bfloat16)
    return upper, (values - upper.astype(jnp.float32)).astype(jnp.bfloat16)


def times(left, right):
    dot = functools.partial(jnp.dot, preferred_element_type=jnp.float32)
    return dot(left[0], right[0]) + dot(left[0], right[1]) + dot(left[1], right[0])


def both(pair_refs):
    return pair_refs[0][...], pair_refs[1][...]


def at(column):
    return slice(column * lanes, (column + 1) * lanes)


def to_columns(parts, orbitals, block, z_up, z_low, y_up, y_low, sent):
    orb_count, slab, rows, _ = orbitals.shape
    share = rows // parts
    stride = sent.shape[0] // parts
    wave_z, wave_y = both((z_up, z_low)), both((y_up, y_low))
    for orb in range(orb_count):
        density = jnp.concatenate([orbitals[orb] * block[0], orbitals[orb] * block[1]], axis=-1)
        spectrum = times(split(density.reshape(slab * rows, 2 * lanes)), wave_z)
        spectrum = spectrum.reshape(slab, rows, 2 * lanes)
        stacked = jnp.concatenate(
            [
                jnp.concatenate([spectrum[plane, :, :lanes], spectrum[plane, :, lanes:]], axis=0)
                for plane in range(slab)
            ],
            axis=1,
        )
        columns = times(wave_y, split(stacked))
        for part in range(2):
            for plane in range(slab):
                first = ((orb * 2 + part) * slab + plane) * share
                for place in range(share):
                    start = (part * share + place) * parts
                    sent[pl.ds(first + place, parts, stride), :] = columns[
                        start : start + parts, at(plane)
                    ]


def in_columns(parts, received, weights, f_up, f_low, i_up, i_low, sent):
    stride = received.shape[0] // parts
    group = f_up.shape[0] // parts
    share = weights.shape[1] // lanes
    forward, inverse = both((f_up, f_low)), both((i_up, i_low))
    scale = jnp.concatenate([weights[...]] * 2, axis=0)
    for orb in range(stride // (group * share)):
        first = orb * group * share
        stacked = jnp.concatenate(
            [
                jnp.concatenate(
                    [
                        received[pl.ds(first + row * share + place, parts, stride), :]
                        for place in range(share)
                    ],
                    axis=1,
                )
                for row in range(group)
            ],
            axis=0,
        )
        spectral = times(forward, split(stacked)) * scale
        planes = times(inverse, split(spectral))
        for row in range(group):
            for place in range(share):
                sent[pl.ds(first + row * share + place, parts, stride), :] = planes[
                    row * parts : (row + 1) * parts, at(place)
                ]


def from_columns(parts, received, block, y_up, y_low, z_up, z_low, out):
    orb_count, slab, rows, _ = out.shape
    share = rows // parts
    stride = received.shape[0] // parts
    wave_y, wave_z = both((y_up, y_low)), both((z_up, z_low))
    for orb in range(orb_count):
        stacked = jnp.concatenate(
            [
                jnp.concatenate(
                    [
                        received[
                            pl.ds(
                                ((orb * 2 + part) * slab + plane) * share + place, parts, stride
                            ),
                            :,
                        ]
                        for part in range(2)
                        for place in range(share)
                    ],
                    axis=0,
                )
                for plane in range(slab)
            ],
            axis=1,
        )
        spectrum = times(wave_y, split(stacked))
        spectrum = jnp.concatenate(
            [
                jnp.concatenate([spectrum[:rows, at(plane)], spectrum[rows:, at(plane)]], axis=1)
                for plane in range(slab)
            ],
            axis=0,
        )
        potential = times(split(spectrum), wave_z).reshape(slab, rows, 2 * lanes)
        out[orb] = block[0] * potential[..., :lanes] + block[1] * potential[..., lanes:]


def on_device(body, shape, flops, *operands):
    moved = sum(x.size * x.dtype.itemsize for x in operands) + 4 * int(np.prod(shape))
    return pl.pallas_call(
        body,
        out_shape=jax.ShapeDtypeStruct(shape, jnp.float32),
        in_specs=[pl.BlockSpec(memory_space=pltpu.VMEM)] * len(operands),
        out_specs=pl.BlockSpec(memory_space=pltpu.VMEM),
        compiler_params=pltpu.CompilerParams(vmem_limit_bytes=32 * 1024 * 1024),
        cost_estimate=pl.CostEstimate(flops=flops, bytes_accessed=moved, transcendentals=0),
    )(*operands)


def local(orbitals, kernel, owners):
    orb_count, slab, rows, cells = orbitals.shape
    parts = lax.axis_size(grid_axes)
    full = slab * parts
    share = rows // parts
    order_x, order_y = spread(full, parts), spread(rows, parts)
    forward_z = halves(wave(cells, True).T)
    inverse_z = halves(wave(cells, False).T * (-mixing / (full * rows * cells)))
    forward_y = halves(wave(rows, True)[order_y])
    inverse_y = halves(wave(rows, False)[:, order_y])
    forward_x = halves(wave(full, True)[order_x][:, order_x])
    inverse_x = halves(wave(full, False)[order_x][:, order_x])
    weights = kernel.reshape(parts, slab, share * cells).swapaxes(0, 1).reshape(full, share * cells)

    source_block, weights = broadcast(orbitals, owners[0], weights)
    sent_rows = orb_count * 2 * slab * share
    shape = (parts * sent_rows, cells)
    points = orb_count * slab * rows * cells

    def exchange(columns):
        columns = columns.reshape(parts, sent_rows, cells)
        return lax.all_to_all(columns, grid_axes, 0, 0, tiled=True).reshape(shape)

    columns = on_device(
        functools.partial(to_columns, parts),
        shape,
        24 * points * (cells + rows),
        orbitals,
        source_block,
        *forward_z,
        *forward_y,
    )
    columns = exchange(columns)
    columns = on_device(
        functools.partial(in_columns, parts),
        shape,
        48 * points * full,
        columns,
        weights,
        *forward_x,
        *inverse_x,
    )
    columns = exchange(columns)
    return on_device(
        functools.partial(from_columns, parts),
        orbitals.shape,
        24 * points * (cells + rows),
        columns,
        source_block,
        *inverse_y,
        *inverse_z,
    )


def solution(mesh):
    band, grid = mesh.shape["band"], mesh.shape["grid"]
    shape = (band // (4 * pair), 4, pair, grid // (2 * pair), pair, 2)
    fine = Mesh(mesh.devices.reshape(shape), band_axes + grid_axes)
    return jax.shard_map(
        local,
        mesh=fine,
        in_specs=(P(band_axes, grid_axes, None, None), P(None, grid_axes, None), P()),
        out_specs=P(band_axes, grid_axes, None, None),
        check_vma=False,
    )
```

```python
import functools

import jax
import jax.numpy as jnp
import numpy as np
from jax import lax
from jax.experimental import pallas as pl
from jax.experimental.pallas import tpu as pltpu
from jax.sharding import Mesh, PartitionSpec as P

mixing = 0.25
pair = 2
far_axis = "z_far"
near_axes = ("z_near", "y_lo")
band_axes = (far_axis,) + near_axes
grid_axes = ("x", "y_hi", "core")
lanes = 128


def pieces_of(block, axes, holder):
    pieces = block.reshape(lax.axis_size(axes), -1, block.shape[-1])
    received = lax.all_to_all(pieces, axes, 0, 0, tiled=True)
    return lax.dynamic_index_in_dim(received, holder, 0, keepdims=False)


def copies_of(piece, axes):
    copies = jnp.broadcast_to(piece[None], (lax.axis_size(axes),) + piece.shape)
    return lax.all_to_all(copies, axes, 0, 0, tiled=True)


def broadcast(block, holder, aside):
    members = lax.axis_size(near_axes)
    flip = near_axes[::-1]
    place = (holder % 2) * (members // 2) + (holder % members) // 2
    piece = pieces_of(block, flip, place)
    piece, aside = lax.optimization_barrier((piece, aside))
    everywhere = lax.all_gather(piece, far_axis, axis=0)
    piece = lax.dynamic_index_in_dim(everywhere, holder // members, 0, keepdims=False)
    return copies_of(piece, flip).reshape(block.shape), aside


def wave(length, forward):
    counter = np.arange(length)
    angles = 2.0 * np.pi * (np.outer(counter, counter) % length) / length
    cosine, sine = np.cos(angles), np.sin(angles)
    if not forward:
        sine = -sine
    return np.block([[cosine, sine], [-sine, cosine]])


def spread(length, parts):
    order = np.arange(length).reshape(parts, -1).T.reshape(-1)
    return np.concatenate([order, order + length])


def halves(matrix):
    upper = matrix.astype(jnp.bfloat16)
    return upper, (matrix - upper.astype(np.float64)).astype(jnp.bfloat16)


def split(values):
    upper = values.astype(jnp.bfloat16)
    return upper, (values - upper.astype(jnp.float32)).astype(jnp.bfloat16)


def times(left, right):
    dot = functools.partial(jnp.dot, preferred_element_type=jnp.float32)
    return dot(left[0], right[0]) + dot(left[0], right[1]) + dot(left[1], right[0])


def both(pair_refs):
    return pair_refs[0][...], pair_refs[1][...]


def at(column):
    return slice(column * lanes, (column + 1) * lanes)


def to_columns(parts, orbitals, block, z_up, z_low, y_up, y_low, sent):
    orb_count, slab, rows, _ = orbitals.shape
    share = rows // parts
    stride = sent.shape[0] // parts
    wave_z, wave_y = both((z_up, z_low)), both((y_up, y_low))
    for orb in range(orb_count):
        density = jnp.concatenate([orbitals[orb] * block[0], orbitals[orb] * block[1]], axis=-1)
        spectrum = times(split(density.reshape(slab * rows, 2 * lanes)), wave_z)
        spectrum = spectrum.reshape(slab, rows, 2 * lanes)
        stacked = jnp.concatenate(
            [
                jnp.concatenate([spectrum[plane, :, :lanes], spectrum[plane, :, lanes:]], axis=0)
                for plane in range(slab)
            ],
            axis=1,
        )
        columns = times(wave_y, split(stacked))
        for part in range(2):
            for plane in range(slab):
                first = ((orb * 2 + part) * slab + plane) * share
                for place in range(share):
                    start = (part * share + place) * parts
                    sent[pl.ds(first + place, parts, stride), :] = columns[
                        start : start + parts, at(plane)
                    ]


def in_columns(parts, received, weights, f_up, f_low, i_up, i_low, sent):
    stride = received.shape[0] // parts
    group = f_up.shape[0] // parts
    share = weights.shape[1] // lanes
    forward, inverse = both((f_up, f_low)), both((i_up, i_low))
    scale = jnp.concatenate([weights[...]] * 2, axis=0)
    for orb in range(stride // (group * share)):
        first = orb * group * share
        stacked = jnp.concatenate(
            [
                jnp.concatenate(
                    [
                        received[pl.ds(first + row * share + place, parts, stride), :]
                        for place in range(share)
                    ],
                    axis=1,
                )
                for row in range(group)
            ],
            axis=0,
        )
        spectral = times(forward, split(stacked)) * scale
        planes = times(inverse, split(spectral))
        for row in range(group):
            for place in range(share):
                sent[pl.ds(first + row * share + place, parts, stride), :] = planes[
                    row * parts : (row + 1) * parts, at(place)
                ]


def from_columns(parts, received, block, y_up, y_low, z_up, z_low, out):
    orb_count, slab, rows, _ = out.shape
    share = rows // parts
    stride = received.shape[0] // parts
    wave_y, wave_z = both((y_up, y_low)), both((z_up, z_low))
    for orb in range(orb_count):
        stacked = jnp.concatenate(
            [
                jnp.concatenate(
                    [
                        received[
                            pl.ds(
                                ((orb * 2 + part) * slab + plane) * share + place, parts, stride
                            ),
                            :,
                        ]
                        for part in range(2)
                        for place in range(share)
                    ],
                    axis=0,
                )
                for plane in range(slab)
            ],
            axis=1,
        )
        spectrum = times(wave_y, split(stacked))
        spectrum = jnp.concatenate(
            [
                jnp.concatenate([spectrum[:rows, at(plane)], spectrum[rows:, at(plane)]], axis=1)
                for plane in range(slab)
            ],
            axis=0,
        )
        potential = times(split(spectrum), wave_z).reshape(slab, rows, 2 * lanes)
        out[orb] = block[0] * potential[..., :lanes] + block[1] * potential[..., lanes:]


def on_device(body, shape, flops, *operands):
    moved = sum(x.size * x.dtype.itemsize for x in operands) + 4 * int(np.prod(shape))
    return pl.pallas_call(
        body,
        out_shape=jax.ShapeDtypeStruct(shape, jnp.float32),
        in_specs=[pl.BlockSpec(memory_space=pltpu.VMEM)] * len(operands),
        out_specs=pl.BlockSpec(memory_space=pltpu.VMEM),
        compiler_params=pltpu.CompilerParams(vmem_limit_bytes=32 * 1024 * 1024),
        cost_estimate=pl.CostEstimate(flops=flops, bytes_accessed=moved, transcendentals=0),
    )(*operands)


def local(orbitals, kernel, owners):
    orb_count, slab, rows, cells = orbitals.shape
    parts = lax.axis_size(grid_axes)
    full = slab * parts
    share = rows // parts
    order_x, order_y = spread(full, parts), spread(rows, parts)
    forward_z = halves(wave(cells, True).T)
    inverse_z = halves(wave(cells, False).T * (-mixing / (full * rows * cells)))
    forward_y = halves(wave(rows, True)[order_y])
    inverse_y = halves(wave(rows, False)[:, order_y])
    forward_x = halves(wave(full, True)[order_x][:, order_x])
    inverse_x = halves(wave(full, False)[order_x][:, order_x])
    weights = kernel.reshape(parts, slab, share * cells).swapaxes(0, 1).reshape(full, share * cells)

    source_block, weights = broadcast(orbitals, owners[0], weights)
    sent_rows = orb_count * 2 * slab * share
    shape = (parts * sent_rows, cells)
    points = orb_count * slab * rows * cells

    def exchange(columns):
        columns = columns.reshape(parts, sent_rows, cells)
        return lax.all_to_all(columns, grid_axes, 0, 0, tiled=True).reshape(shape)

    columns = on_device(
        functools.partial(to_columns, parts),
        shape,
        24 * points * (cells + rows),
        orbitals,
        source_block,
        *forward_z,
        *forward_y,
    )
    columns = exchange(columns)
    columns = on_device(
        functools.partial(in_columns, parts),
        shape,
        48 * points * full,
        columns,
        weights,
        *forward_x,
        *inverse_x,
    )
    columns = exchange(columns)
    return on_device(
        functools.partial(from_columns, parts),
        orbitals.shape,
        24 * points * (cells + rows),
        columns,
        source_block,
        *inverse_y,
        *inverse_z,
    )


def solution(mesh):
    band, grid = mesh.shape["band"], mesh.shape["grid"]
    shape = (band // (4 * pair), 4, pair, grid // (2 * pair), pair, 2)
    fine = Mesh(mesh.devices.reshape(shape), band_axes + grid_axes)
    return jax.shard_map(
        local,
        mesh=fine,
        in_specs=(P(band_axes, grid_axes, None, None), P(None, grid_axes, None), P()),
        out_specs=P(band_axes, grid_axes, None, None),
        check_vma=False,
    )
```

```python
import functools

import jax
import jax.numpy as jnp
import numpy as np
from jax import lax
from jax.experimental import pallas as pl
from jax.experimental.pallas import tpu as pltpu
from jax.sharding import Mesh, PartitionSpec as P

mixing = 0.25
pair = 2
far_axis = "z_far"
near_axes = ("z_near", "y_lo")
band_axes = (far_axis,) + near_axes
grid_axes = ("x", "y_hi", "core")
lanes = 128


def pieces_of(block, axes, holder):
    pieces = block.reshape(lax.axis_size(axes), -1, block.shape[-1])
    received = lax.all_to_all(pieces, axes, 0, 0, tiled=True)
    return lax.dynamic_index_in_dim(received, holder, 0, keepdims=False)


def copies_of(piece, axes):
    copies = jnp.broadcast_to(piece[None], (lax.axis_size(axes),) + piece.shape)
    return lax.all_to_all(copies, axes, 0, 0, tiled=True)


def far_copies(piece, source):
    count = lax.axis_size(far_axis)
    mine = lax.axis_index(far_axis)
    order = sorted(range(count), key=lambda place: min(place, count - place))

    def sent_by(first):
        def send(piece):
            result = piece
            for target in order:
                if target != first:
                    got = lax.ppermute(piece, far_axis, [(first, target)])
                    result = jnp.where(mine == target, got, result)
            return result

        return send

    return lax.switch(source, [sent_by(first) for first in range(count)], piece)


def broadcast(block, holder, aside):
    members = lax.axis_size(near_axes)
    flip = near_axes[::-1]
    place = (holder % 2) * (members // 2) + (holder % members) // 2
    piece = pieces_of(block, flip, place)
    piece, aside = lax.optimization_barrier((piece, aside))
    piece = far_copies(piece, holder // members)
    return copies_of(piece, flip).reshape(block.shape), aside


def wave(length, forward):
    counter = np.arange(length)
    angles = 2.0 * np.pi * (np.outer(counter, counter) % length) / length
    cosine, sine = np.cos(angles), np.sin(angles)
    if not forward:
        sine = -sine
    return np.block([[cosine, sine], [-sine, cosine]])


def spread(length, parts):
    order = np.arange(length).reshape(parts, -1).T.reshape(-1)
    return np.concatenate([order, order + length])


def halves(matrix):
    upper = matrix.astype(jnp.bfloat16)
    return upper, (matrix - upper.astype(np.float64)).astype(jnp.bfloat16)


def split(values):
    upper = values.astype(jnp.bfloat16)
    return upper, (values - upper.astype(jnp.float32)).astype(jnp.bfloat16)


def times(left, right):
    dot = functools.partial(jnp.dot, preferred_element_type=jnp.float32)
    return dot(left[0], right[0]) + dot(left[0], right[1]) + dot(left[1], right[0])


def both(pair_refs):
    return pair_refs[0][...], pair_refs[1][...]


def at(column):
    return slice(column * lanes, (column + 1) * lanes)


def to_columns(parts, orbitals, block, z_up, z_low, y_up, y_low, sent):
    orb_count, slab, rows, _ = orbitals.shape
    share = rows // parts
    stride = sent.shape[0] // parts
    wave_z, wave_y = both((z_up, z_low)), both((y_up, y_low))
    for orb in range(orb_count):
        density = jnp.concatenate([orbitals[orb] * block[0], orbitals[orb] * block[1]], axis=-1)
        spectrum = times(split(density.reshape(slab * rows, 2 * lanes)), wave_z)
        spectrum = spectrum.reshape(slab, rows, 2 * lanes)
        stacked = jnp.concatenate(
            [
                jnp.concatenate([spectrum[plane, :, :lanes], spectrum[plane, :, lanes:]], axis=0)
                for plane in range(slab)
            ],
            axis=1,
        )
        columns = times(wave_y, split(stacked))
        for part in range(2):
            for plane in range(slab):
                first = ((orb * 2 + part) * slab + plane) * share
                for place in range(share):
                    start = (part * share + place) * parts
                    sent[pl.ds(first + place, parts, stride), :] = columns[
                        start : start + parts, at(plane)
                    ]


def in_columns(parts, received, weights, f_up, f_low, i_up, i_low, sent):
    stride = received.shape[0] // parts
    group = f_up.shape[0] // parts
    share = weights.shape[1] // lanes
    forward, inverse = both((f_up, f_low)), both((i_up, i_low))
    scale = jnp.concatenate([weights[...]] * 2, axis=0)
    for orb in range(stride // (group * share)):
        first = orb * group * share
        stacked = jnp.concatenate(
            [
                jnp.concatenate(
                    [
                        received[pl.ds(first + row * share + place, parts, stride), :]
                        for place in range(share)
                    ],
                    axis=1,
                )
                for row in range(group)
            ],
            axis=0,
        )
        spectral = times(forward, split(stacked)) * scale
        planes = times(inverse, split(spectral))
        for row in range(group):
            for place in range(share):
                sent[pl.ds(first + row * share + place, parts, stride), :] = planes[
                    row * parts : (row + 1) * parts, at(place)
                ]


def from_columns(parts, received, block, y_up, y_low, z_up, z_low, out):
    orb_count, slab, rows, _ = out.shape
    share = rows // parts
    stride = received.shape[0] // parts
    wave_y, wave_z = both((y_up, y_low)), both((z_up, z_low))
    for orb in range(orb_count):
        stacked = jnp.concatenate(
            [
                jnp.concatenate(
                    [
                        received[
                            pl.ds(
                                ((orb * 2 + part) * slab + plane) * share + place, parts, stride
                            ),
                            :,
                        ]
                        for part in range(2)
                        for place in range(share)
                    ],
                    axis=0,
                )
                for plane in range(slab)
            ],
            axis=1,
        )
        spectrum = times(wave_y, split(stacked))
        spectrum = jnp.concatenate(
            [
                jnp.concatenate([spectrum[:rows, at(plane)], spectrum[rows:, at(plane)]], axis=1)
                for plane in range(slab)
            ],
            axis=0,
        )
        potential = times(split(spectrum), wave_z).reshape(slab, rows, 2 * lanes)
        out[orb] = block[0] * potential[..., :lanes] + block[1] * potential[..., lanes:]


def on_device(body, shape, flops, *operands):
    moved = sum(x.size * x.dtype.itemsize for x in operands) + 4 * int(np.prod(shape))
    return pl.pallas_call(
        body,
        out_shape=jax.ShapeDtypeStruct(shape, jnp.float32),
        in_specs=[pl.BlockSpec(memory_space=pltpu.VMEM)] * len(operands),
        out_specs=pl.BlockSpec(memory_space=pltpu.VMEM),
        compiler_params=pltpu.CompilerParams(vmem_limit_bytes=32 * 1024 * 1024),
        cost_estimate=pl.CostEstimate(flops=flops, bytes_accessed=moved, transcendentals=0),
    )(*operands)


def local(orbitals, kernel, owners):
    orb_count, slab, rows, cells = orbitals.shape
    parts = lax.axis_size(grid_axes)
    full = slab * parts
    share = rows // parts
    order_x, order_y = spread(full, parts), spread(rows, parts)
    forward_z = halves(wave(cells, True).T)
    inverse_z = halves(wave(cells, False).T * (-mixing / (full * rows * cells)))
    forward_y = halves(wave(rows, True)[order_y])
    inverse_y = halves(wave(rows, False)[:, order_y])
    forward_x = halves(wave(full, True)[order_x][:, order_x])
    inverse_x = halves(wave(full, False)[order_x][:, order_x])
    weights = kernel.reshape(parts, slab, share * cells).swapaxes(0, 1).reshape(full, share * cells)

    source_block, weights = broadcast(orbitals, owners[0], weights)
    sent_rows = orb_count * 2 * slab * share
    shape = (parts * sent_rows, cells)
    points = orb_count * slab * rows * cells

    def exchange(columns):
        columns = columns.reshape(parts, sent_rows, cells)
        return lax.all_to_all(columns, grid_axes, 0, 0, tiled=True).reshape(shape)

    columns = on_device(
        functools.partial(to_columns, parts),
        shape,
        24 * points * (cells + rows),
        orbitals,
        source_block,
        *forward_z,
        *forward_y,
    )
    columns = exchange(columns)
    columns = on_device(
        functools.partial(in_columns, parts),
        shape,
        48 * points * full,
        columns,
        weights,
        *forward_x,
        *inverse_x,
    )
    columns = exchange(columns)
    return on_device(
        functools.partial(from_columns, parts),
        orbitals.shape,
        24 * points * (cells + rows),
        columns,
        source_block,
        *inverse_y,
        *inverse_z,
    )


def solution(mesh):
    band, grid = mesh.shape["band"], mesh.shape["grid"]
    shape = (band // (4 * pair), 4, pair, grid // (2 * pair), pair, 2)
    fine = Mesh(mesh.devices.reshape(shape), band_axes + grid_axes)
    return jax.shard_map(
        local,
        mesh=fine,
        in_specs=(P(band_axes, grid_axes, None, None), P(None, grid_axes, None), P()),
        out_specs=P(band_axes, grid_axes, None, None),
        check_vma=False,
    )
```

```python
import functools

import jax
import jax.numpy as jnp
import numpy as np
from jax import lax
from jax.experimental import pallas as pl
from jax.experimental.pallas import tpu as pltpu
from jax.sharding import Mesh, PartitionSpec as P

mixing = 0.25
pair = 2
far_axis = "z_far"
near_axes = ("z_near", "y_lo")
band_axes = (far_axis,) + near_axes
grid_axes = ("x", "y_hi", "core")
lanes = 128


def pieces_of(block, axes, holder):
    pieces = block.reshape(lax.axis_size(axes), -1, block.shape[-1])
    received = lax.all_to_all(pieces, axes, 0, 0, tiled=True)
    return lax.dynamic_index_in_dim(received, holder, 0, keepdims=False)


def copies_of(piece, axes):
    copies = jnp.broadcast_to(piece[None], (lax.axis_size(axes),) + piece.shape)
    return lax.all_to_all(copies, axes, 0, 0, tiled=True)


def far_copies(piece, source):
    count = lax.axis_size(far_axis)
    mine = lax.axis_index(far_axis)
    order = sorted(range(count), key=lambda place: min(place, count - place))

    def sent_by(first):
        def send(piece):
            result = piece
            for target in order:
                if target != first:
                    got = lax.ppermute(piece, far_axis, [(first, target)])
                    result = jnp.where(mine == target, got, result)
            return result

        return send

    return lax.switch(source, [sent_by(first) for first in range(count)], piece)


def broadcast(block, holder, aside):
    members = lax.axis_size(near_axes)
    flip = near_axes[::-1]
    place = (holder % 2) * (members // 2) + (holder % members) // 2
    piece = pieces_of(block, flip, place)
    piece, aside = lax.optimization_barrier((piece, aside))
    piece = far_copies(piece, holder // members)
    piece, aside = lax.optimization_barrier((piece, aside))
    return copies_of(piece, flip).reshape(block.shape), aside


def wave(length, forward):
    counter = np.arange(length)
    angles = 2.0 * np.pi * (np.outer(counter, counter) % length) / length
    cosine, sine = np.cos(angles), np.sin(angles)
    if not forward:
        sine = -sine
    return np.block([[cosine, sine], [-sine, cosine]])


def spread(length, parts):
    order = np.arange(length).reshape(parts, -1).T.reshape(-1)
    return np.concatenate([order, order + length])


def halves(matrix):
    upper = matrix.astype(jnp.bfloat16)
    return upper, (matrix - upper.astype(np.float64)).astype(jnp.bfloat16)


def split(values):
    upper = values.astype(jnp.bfloat16)
    return upper, (values - upper.astype(jnp.float32)).astype(jnp.bfloat16)


def times(left, right):
    dot = functools.partial(jnp.dot, preferred_element_type=jnp.float32)
    return dot(left[0], right[0]) + dot(left[0], right[1]) + dot(left[1], right[0])


def both(pair_refs):
    return pair_refs[0][...], pair_refs[1][...]


def at(column):
    return slice(column * lanes, (column + 1) * lanes)


def to_columns(parts, orbitals, block, z_up, z_low, y_up, y_low, sent):
    orb_count, slab, rows, _ = orbitals.shape
    share = rows // parts
    stride = sent.shape[0] // parts
    wave_z, wave_y = both((z_up, z_low)), both((y_up, y_low))
    for orb in range(orb_count):
        density = jnp.concatenate([orbitals[orb] * block[0], orbitals[orb] * block[1]], axis=-1)
        spectrum = times(split(density.reshape(slab * rows, 2 * lanes)), wave_z)
        spectrum = spectrum.reshape(slab, rows, 2 * lanes)
        stacked = jnp.concatenate(
            [
                jnp.concatenate([spectrum[plane, :, :lanes], spectrum[plane, :, lanes:]], axis=0)
                for plane in range(slab)
            ],
            axis=1,
        )
        columns = times(wave_y, split(stacked))
        for part in range(2):
            for plane in range(slab):
                first = ((orb * 2 + part) * slab + plane) * share
                for place in range(share):
                    start = (part * share + place) * parts
                    sent[pl.ds(first + place, parts, stride), :] = columns[
                        start : start + parts, at(plane)
                    ]


def in_columns(parts, received, weights, f_up, f_low, i_up, i_low, sent):
    stride = received.shape[0] // parts
    group = f_up.shape[0] // parts
    share = weights.shape[1] // lanes
    forward, inverse = both((f_up, f_low)), both((i_up, i_low))
    scale = jnp.concatenate([weights[...]] * 2, axis=0)
    for orb in range(stride // (group * share)):
        first = orb * group * share
        stacked = jnp.concatenate(
            [
                jnp.concatenate(
                    [
                        received[pl.ds(first + row * share + place, parts, stride), :]
                        for place in range(share)
                    ],
                    axis=1,
                )
                for row in range(group)
            ],
            axis=0,
        )
        spectral = times(forward, split(stacked)) * scale
        planes = times(inverse, split(spectral))
        for row in range(group):
            for place in range(share):
                sent[pl.ds(first + row * share + place, parts, stride), :] = planes[
                    row * parts : (row + 1) * parts, at(place)
                ]


def from_columns(parts, received, block, y_up, y_low, z_up, z_low, out):
    orb_count, slab, rows, _ = out.shape
    share = rows // parts
    stride = received.shape[0] // parts
    wave_y, wave_z = both((y_up, y_low)), both((z_up, z_low))
    for orb in range(orb_count):
        stacked = jnp.concatenate(
            [
                jnp.concatenate(
                    [
                        received[
                            pl.ds(
                                ((orb * 2 + part) * slab + plane) * share + place, parts, stride
                            ),
                            :,
                        ]
                        for part in range(2)
                        for place in range(share)
                    ],
                    axis=0,
                )
                for plane in range(slab)
            ],
            axis=1,
        )
        spectrum = times(wave_y, split(stacked))
        spectrum = jnp.concatenate(
            [
                jnp.concatenate([spectrum[:rows, at(plane)], spectrum[rows:, at(plane)]], axis=1)
                for plane in range(slab)
            ],
            axis=0,
        )
        potential = times(split(spectrum), wave_z).reshape(slab, rows, 2 * lanes)
        out[orb] = block[0] * potential[..., :lanes] + block[1] * potential[..., lanes:]


def on_device(body, shape, flops, *operands):
    moved = sum(x.size * x.dtype.itemsize for x in operands) + 4 * int(np.prod(shape))
    return pl.pallas_call(
        body,
        out_shape=jax.ShapeDtypeStruct(shape, jnp.float32),
        in_specs=[pl.BlockSpec(memory_space=pltpu.VMEM)] * len(operands),
        out_specs=pl.BlockSpec(memory_space=pltpu.VMEM),
        compiler_params=pltpu.CompilerParams(vmem_limit_bytes=32 * 1024 * 1024),
        cost_estimate=pl.CostEstimate(flops=flops, bytes_accessed=moved, transcendentals=0),
    )(*operands)


def local(orbitals, kernel, owners):
    orb_count, slab, rows, cells = orbitals.shape
    parts = lax.axis_size(grid_axes)
    full = slab * parts
    share = rows // parts
    order_x, order_y = spread(full, parts), spread(rows, parts)
    forward_z = halves(wave(cells, True).T)
    inverse_z = halves(wave(cells, False).T * (-mixing / (full * rows * cells)))
    forward_y = halves(wave(rows, True)[order_y])
    inverse_y = halves(wave(rows, False)[:, order_y])
    forward_x = halves(wave(full, True)[order_x][:, order_x])
    inverse_x = halves(wave(full, False)[order_x][:, order_x])
    weights = kernel.reshape(parts, slab, share * cells).swapaxes(0, 1).reshape(full, share * cells)

    source_block, weights = broadcast(orbitals, owners[0], weights)
    sent_rows = orb_count * 2 * slab * share
    shape = (parts * sent_rows, cells)
    points = orb_count * slab * rows * cells

    def exchange(columns):
        columns = columns.reshape(parts, sent_rows, cells)
        return lax.all_to_all(columns, grid_axes, 0, 0, tiled=True).reshape(shape)

    columns = on_device(
        functools.partial(to_columns, parts),
        shape,
        24 * points * (cells + rows),
        orbitals,
        source_block,
        *forward_z,
        *forward_y,
    )
    columns = exchange(columns)
    columns = on_device(
        functools.partial(in_columns, parts),
        shape,
        48 * points * full,
        columns,
        weights,
        *forward_x,
        *inverse_x,
    )
    columns = exchange(columns)
    return on_device(
        functools.partial(from_columns, parts),
        orbitals.shape,
        24 * points * (cells + rows),
        columns,
        source_block,
        *inverse_y,
        *inverse_z,
    )


def solution(mesh):
    band, grid = mesh.shape["band"], mesh.shape["grid"]
    shape = (band // (4 * pair), 4, pair, grid // (2 * pair), pair, 2)
    fine = Mesh(mesh.devices.reshape(shape), band_axes + grid_axes)
    return jax.shard_map(
        local,
        mesh=fine,
        in_specs=(P(band_axes, grid_axes, None, None), P(None, grid_axes, None), P()),
        out_specs=P(band_axes, grid_axes, None, None),
        check_vma=False,
    )
```

```python
import functools

import jax
import jax.numpy as jnp
import numpy as np
from jax import lax
from jax.experimental import pallas as pl
from jax.experimental.pallas import tpu as pltpu
from jax.sharding import Mesh, PartitionSpec as P

mixing = 0.25
pair = 2
far_axis = "z_far"
near_axes = ("z_near", "y_lo")
band_axes = (far_axis,) + near_axes
grid_axes = ("x", "y_hi", "core")
lanes = 128


def pieces_of(block, axes, holder):
    pieces = block.reshape(lax.axis_size(axes), -1, block.shape[-1])
    received = lax.all_to_all(pieces, axes, 0, 0, tiled=True)
    return lax.dynamic_index_in_dim(received, holder, 0, keepdims=False)


def copies_of(piece, axes):
    copies = jnp.broadcast_to(piece[None], (lax.axis_size(axes),) + piece.shape)
    return lax.all_to_all(copies, axes, 0, 0, tiled=True)


def far_copies(piece, source):
    count = lax.axis_size(far_axis)
    mine = lax.axis_index(far_axis)
    order = sorted(range(count), key=lambda place: min(place, count - place))

    def sent_by(first):
        def send(piece):
            result = piece
            for target in order:
                if target != first:
                    got = lax.ppermute(piece, far_axis, [(first, target)])
                    result = jnp.where(mine == target, got, result)
            return result

        return send

    return lax.switch(source, [sent_by(first) for first in range(count)], piece)


def broadcast(block, holder, aside):
    members = lax.axis_size(near_axes)
    flip = near_axes[::-1]
    place = (holder % 2) * (members // 2) + (holder % members) // 2
    source = holder // members
    piece = lax.cond(
        (source > 0) | (lax.axis_index(far_axis) == source),
        lambda block: pieces_of(block, flip, place),
        lambda block: jnp.zeros((block.size // (members * lanes), lanes), block.dtype),
        block,
    )
    piece, aside = lax.optimization_barrier((piece, aside))
    piece = far_copies(piece, holder // members)
    piece, aside = lax.optimization_barrier((piece, aside))
    return copies_of(piece, flip).reshape(block.shape), aside


def wave(length, forward):
    counter = np.arange(length)
    angles = 2.0 * np.pi * (np.outer(counter, counter) % length) / length
    cosine, sine = np.cos(angles), np.sin(angles)
    if not forward:
        sine = -sine
    return np.block([[cosine, sine], [-sine, cosine]])


def spread(length, parts):
    order = np.arange(length).reshape(parts, -1).T.reshape(-1)
    return np.concatenate([order, order + length])


def halves(matrix):
    upper = matrix.astype(jnp.bfloat16)
    return upper, (matrix - upper.astype(np.float64)).astype(jnp.bfloat16)


def split(values):
    upper = values.astype(jnp.bfloat16)
    return upper, (values - upper.astype(jnp.float32)).astype(jnp.bfloat16)


def times(left, right):
    dot = functools.partial(jnp.dot, preferred_element_type=jnp.float32)
    return dot(left[0], right[0]) + dot(left[0], right[1]) + dot(left[1], right[0])


def both(pair_refs):
    return pair_refs[0][...], pair_refs[1][...]


def at(column):
    return slice(column * lanes, (column + 1) * lanes)


def to_columns(parts, orbitals, block, z_up, z_low, y_up, y_low, sent):
    orb_count, slab, rows, _ = orbitals.shape
    share = rows // parts
    stride = sent.shape[0] // parts
    wave_z, wave_y = both((z_up, z_low)), both((y_up, y_low))
    for orb in range(orb_count):
        density = jnp.concatenate([orbitals[orb] * block[0], orbitals[orb] * block[1]], axis=-1)
        spectrum = times(split(density.reshape(slab * rows, 2 * lanes)), wave_z)
        spectrum = spectrum.reshape(slab, rows, 2 * lanes)
        stacked = jnp.concatenate(
            [
                jnp.concatenate([spectrum[plane, :, :lanes], spectrum[plane, :, lanes:]], axis=0)
                for plane in range(slab)
            ],
            axis=1,
        )
        columns = times(wave_y, split(stacked))
        for part in range(2):
            for plane in range(slab):
                first = ((orb * 2 + part) * slab + plane) * share
                for place in range(share):
                    start = (part * share + place) * parts
                    sent[pl.ds(first + place, parts, stride), :] = columns[
                        start : start + parts, at(plane)
                    ]


def in_columns(parts, received, weights, f_up, f_low, i_up, i_low, sent):
    stride = received.shape[0] // parts
    group = f_up.shape[0] // parts
    share = weights.shape[1] // lanes
    forward, inverse = both((f_up, f_low)), both((i_up, i_low))
    scale = jnp.concatenate([weights[...]] * 2, axis=0)
    for orb in range(stride // (group * share)):
        first = orb * group * share
        stacked = jnp.concatenate(
            [
                jnp.concatenate(
                    [
                        received[pl.ds(first + row * share + place, parts, stride), :]
                        for place in range(share)
                    ],
                    axis=1,
                )
                for row in range(group)
            ],
            axis=0,
        )
        spectral = times(forward, split(stacked)) * scale
        planes = times(inverse, split(spectral))
        for row in range(group):
            for place in range(share):
                sent[pl.ds(first + row * share + place, parts, stride), :] = planes[
                    row * parts : (row + 1) * parts, at(place)
                ]


def from_columns(parts, received, block, y_up, y_low, z_up, z_low, out):
    orb_count, slab, rows, _ = out.shape
    share = rows // parts
    stride = received.shape[0] // parts
    wave_y, wave_z = both((y_up, y_low)), both((z_up, z_low))
    for orb in range(orb_count):
        stacked = jnp.concatenate(
            [
                jnp.concatenate(
                    [
                        received[
                            pl.ds(
                                ((orb * 2 + part) * slab + plane) * share + place, parts, stride
                            ),
                            :,
                        ]
                        for part in range(2)
                        for place in range(share)
                    ],
                    axis=0,
                )
                for plane in range(slab)
            ],
            axis=1,
        )
        spectrum = times(wave_y, split(stacked))
        spectrum = jnp.concatenate(
            [
                jnp.concatenate([spectrum[:rows, at(plane)], spectrum[rows:, at(plane)]], axis=1)
                for plane in range(slab)
            ],
            axis=0,
        )
        potential = times(split(spectrum), wave_z).reshape(slab, rows, 2 * lanes)
        out[orb] = block[0] * potential[..., :lanes] + block[1] * potential[..., lanes:]


def on_device(body, shape, flops, *operands):
    moved = sum(x.size * x.dtype.itemsize for x in operands) + 4 * int(np.prod(shape))
    return pl.pallas_call(
        body,
        out_shape=jax.ShapeDtypeStruct(shape, jnp.float32),
        in_specs=[pl.BlockSpec(memory_space=pltpu.VMEM)] * len(operands),
        out_specs=pl.BlockSpec(memory_space=pltpu.VMEM),
        compiler_params=pltpu.CompilerParams(vmem_limit_bytes=32 * 1024 * 1024),
        cost_estimate=pl.CostEstimate(flops=flops, bytes_accessed=moved, transcendentals=0),
    )(*operands)


def local(orbitals, kernel, owners):
    orb_count, slab, rows, cells = orbitals.shape
    parts = lax.axis_size(grid_axes)
    full = slab * parts
    share = rows // parts
    order_x, order_y = spread(full, parts), spread(rows, parts)
    forward_z = halves(wave(cells, True).T)
    inverse_z = halves(wave(cells, False).T * (-mixing / (full * rows * cells)))
    forward_y = halves(wave(rows, True)[order_y])
    inverse_y = halves(wave(rows, False)[:, order_y])
    forward_x = halves(wave(full, True)[order_x][:, order_x])
    inverse_x = halves(wave(full, False)[order_x][:, order_x])
    weights = kernel.reshape(parts, slab, share * cells).swapaxes(0, 1).reshape(full, share * cells)

    source_block, weights = broadcast(orbitals, owners[0], weights)
    sent_rows = orb_count * 2 * slab * share
    shape = (parts * sent_rows, cells)
    points = orb_count * slab * rows * cells

    def exchange(columns):
        columns = columns.reshape(parts, sent_rows, cells)
        return lax.all_to_all(columns, grid_axes, 0, 0, tiled=True).reshape(shape)

    columns = on_device(
        functools.partial(to_columns, parts),
        shape,
        24 * points * (cells + rows),
        orbitals,
        source_block,
        *forward_z,
        *forward_y,
    )
    columns = exchange(columns)
    columns = on_device(
        functools.partial(in_columns, parts),
        shape,
        48 * points * full,
        columns,
        weights,
        *forward_x,
        *inverse_x,
    )
    columns = exchange(columns)
    return on_device(
        functools.partial(from_columns, parts),
        orbitals.shape,
        24 * points * (cells + rows),
        columns,
        source_block,
        *inverse_y,
        *inverse_z,
    )


def solution(mesh):
    band, grid = mesh.shape["band"], mesh.shape["grid"]
    shape = (band // (4 * pair), 4, pair, grid // (2 * pair), pair, 2)
    fine = Mesh(mesh.devices.reshape(shape), band_axes + grid_axes)
    return jax.shard_map(
        local,
        mesh=fine,
        in_specs=(P(band_axes, grid_axes, None, None), P(None, grid_axes, None), P()),
        out_specs=P(band_axes, grid_axes, None, None),
        check_vma=False,
    )
```
